128 devices in a mesh: scen: 4 (over y), row: 4 (over x), col: 8 (over z, core).
Axes of the slice: x: 4, y: 4, z: 4, core: 2. Of those that a mesh axis runs over, the one named last changes fastest.
Arguments:
- tech_matrix: bfloat16 [8, 8192, 4096], P('scen', 'row', 'col'), may hold values from -0.02734375 to 0.02734375
- recourse_matrix: bfloat16 [8, 8192, 12288], P('scen', 'row', 'col'), may hold values from -0.02734375 to 0.02734375
- first_cost: float32 [4096], P('col'), may hold values from -60 to 60
- recourse_cost: float32 [8, 12288], P('scen', 'col'), may hold values from -60 to 60
- demand: float32 [8, 8192], P('scen', 'row'), may hold values from -60 to 60
- first_upper: float32 [4096], P('col'), may hold values from 0.5 to 4
- recourse_upper: float32 [8, 12288], P('scen', 'col'), may hold values from 0.5 to 4
- first_start: float32 [4096], P('col'), may hold values from 0 to 1
- recourse_start: float32 [8, 12288], P('scen', 'col'), may hold values from 0 to 1
- dual_start: float32 [8, 8192], P('scen', 'row'), may hold values from 0 to 1
Outputs:
- first_section: float32 [4096], P('col')
- recourse: float32 [8, 12288], P('scen', 'col')
- duals: float32 [8, 8192], P('scen', 'row')
- primal_weight: float32 [], replicated
The draws below stay inside these ranges and needn't reach their ends.
All inputs are finite; a program needn't handle non-finite values.
Results may differ from the reference program's by a relative error of at most 0.0003.
Values sent between devices are 32-bit elements; how exact they have to be, the bound alone decides.
A program may use at most 64 MiB of HBM per device.

```python
import math
import jax
import jax.numpy as jnp
from jax import lax

SCEN = 8
ROWS = 8192
FIRST = 4096
RECOURSE = 12288
ITERS = 4


def rising(count, top):
    return top ** (jnp.arange(count, dtype=jnp.float32) / max(count - 1, 1))


def roughness(key, shape):
    return jnp.exp(jax.random.uniform(key, shape, jnp.float32, math.log(0.5), math.log(2.0)))


def draw_first_cost(key, part):
    key = jax.random.fold_in(key, 11)
    base_key, rough_key = jax.random.split(key)
    base = jax.random.normal(base_key, (FIRST,), jnp.float32)
    top = 3.0
    return jnp.clip(base * roughness(rough_key, (FIRST,)) * rising(FIRST, top), -60.0, 60.0)


def draw_recourse_cost(key, part):
    key = jax.random.fold_in(key, 23)
    base_key, rough_key = jax.random.split(key)
    base = jax.random.normal(base_key, (SCEN, RECOURSE), jnp.float32)
    top = 3.0
    scale = rising(SCEN, 3.0)[:, None] * rising(RECOURSE, top)[None, :]
    return jnp.clip(base * roughness(rough_key, (SCEN, RECOURSE)) * scale, -60.0, 60.0)


def draw_demand(key, part):
    key = jax.random.fold_in(key, 37)
    base_key, rough_key = jax.random.split(key)
    base = jax.random.normal(base_key, (SCEN, ROWS), jnp.float32) + 0.5
    top = 3.0
    scale = rising(SCEN, 3.0)[:, None] * rising(ROWS, top)[None, :]
    return jnp.clip(base * roughness(rough_key, (SCEN, ROWS)) * scale, -60.0, 60.0)


def block_scale(stream_key, extent, cuts, smallest, largest):
    def one(axis_at, parts):
        heights = jax.random.uniform(jax.random.fold_in(jax.random.fold_in(stream_key, 6), axis_at), (parts,), jnp.float32, smallest / len(cuts), largest / len(cuts))
        return jnp.repeat(jnp.exp(heights), extent[axis_at] // parts).reshape((-1,) + (1,) * (len(extent) - axis_at - 1))

    gain = one(*cuts[0])
    for cut in cuts[1:]:
        gain = gain * one(*cut)
    return gain


def centred(rng, shape, scale, limit, cuts=(), kind=jnp.bfloat16):
    array = jax.random.normal(rng, shape, jnp.float32) * scale
    if len(cuts) > 0:
        array = block_scale(rng, shape, cuts, -0.22, 0.18) * array
    return jnp.clip(array, min=-limit, max=limit).astype(kind)


def setup_inputs(seed: int = 0) -> dict:
    keys = jax.random.split(jax.random.key(seed), 11)
    return {
        "tech_matrix": centred(keys[0], (SCEN, ROWS, FIRST), ((ROWS ** 0.5 + (FIRST + RECOURSE) ** 0.5) ** 2) ** -0.5, 0.02734375, ((0, 4), (1, 4), (2, 8))),
        "recourse_matrix": centred(keys[1], (SCEN, ROWS, RECOURSE), ((ROWS ** 0.5 + (FIRST + RECOURSE) ** 0.5) ** 2) ** -0.5, 0.02734375, ((0, 4), (1, 4), (2, 8))),
        "first_cost": draw_first_cost(jax.random.fold_in(keys[10], 71), 0),
        "recourse_cost": draw_recourse_cost(jax.random.fold_in(keys[10], 71), 0),
        "demand": draw_demand(jax.random.fold_in(keys[10], 71), 0),
        "first_upper": jnp.clip(jnp.exp(math.log(4.0) - 2.0794415 * jax.random.uniform(keys[5], (FIRST,), jnp.float32) ** block_scale(keys[5], (FIRST,), ((0, 8),), -0.2, 0.2)), 0.5, 4.0),
        "recourse_upper": jnp.clip(jnp.exp(math.log(4.0) - 2.0794415 * jax.random.uniform(keys[6], (SCEN, RECOURSE), jnp.float32) ** block_scale(keys[6], (SCEN, RECOURSE), ((0, 4), (1, 8)), -0.2, 0.2)), 0.5, 4.0),
        "first_start": jnp.clip(1.0 * jax.random.uniform(keys[7], (FIRST,), jnp.float32) ** block_scale(keys[7], (FIRST,), ((0, 8),), -0.2, 0.2), 0.0, 1.0),
        "recourse_start": jnp.clip(1.0 * jax.random.uniform(keys[8], (SCEN, RECOURSE), jnp.float32) ** block_scale(keys[8], (SCEN, RECOURSE), ((0, 4), (1, 8)), -0.2, 0.2), 0.0, 1.0),
        "dual_start": jnp.clip(1.0 * jax.random.uniform(keys[9], (SCEN, ROWS), jnp.float32) ** block_scale(keys[9], (SCEN, ROWS), ((0, 4), (1, 4)), -0.2, 0.2), 0.0, 1.0),
    }


STEP_SCALE = 0.8
EPSILON = 1e-6


def split_pair(vector):
    upper_part = lax.optimization_barrier(vector.astype(jnp.bfloat16))
    lower_part = (vector - upper_part.astype(vector.dtype)).astype(jnp.bfloat16)
    return upper_part, lower_part


def forward(matrix, vector):
    upper_part, lower_part = split_pair(vector)

    def single(items):
        block, top_vec, low_vec = items
        stacked = jnp.stack([top_vec, low_vec], 1)
        return jnp.dot(block, stacked, preferred_element_type=jnp.float32).sum(1)

    return lax.map(single, (matrix, upper_part, lower_part))


def backward(matrix, vector):
    upper_part, lower_part = split_pair(vector)

    def single(items):
        block, top_vec, low_vec = items
        stacked = jnp.stack([top_vec, low_vec], 0)
        return jnp.dot(stacked, block, preferred_element_type=jnp.float32).sum(0)

    return lax.map(single, (matrix, upper_part, lower_part))


def reference(tech_matrix, recourse_matrix, first_cost, recourse_cost, demand, first_upper, recourse_upper, first_start, recourse_start, dual_start):
    first_now = first_start
    recourse_now = recourse_start
    duals_now = dual_start
    weight_now = jnp.ones((), first_start.dtype)
    for counter in range(ITERS):
        step_primal = STEP_SCALE / weight_now
        step_dual = STEP_SCALE * weight_now
        first_grad = backward(tech_matrix, duals_now).sum(0)
        recourse_grad = backward(recourse_matrix, duals_now)
        first_new = jnp.clip(first_now - step_primal * (first_cost - first_grad), 0.0, first_upper)
        recourse_new = jnp.clip(recourse_now - step_primal * (recourse_cost - recourse_grad), 0.0, recourse_upper)
        first_bar = 2.0 * first_new - first_now
        recourse_bar = 2.0 * recourse_new - recourse_now
        first_wide = jnp.broadcast_to(first_bar, (duals_now.shape[0], first_bar.shape[0]))
        activity = forward(tech_matrix, first_wide) + forward(recourse_matrix, recourse_bar)
        duals_new = jnp.maximum(0.0, duals_now + step_dual * (demand - activity))
        primal_move = jnp.sum((first_new - first_now) ** 2) + jnp.sum((recourse_new - recourse_now) ** 2)
        dual_move = jnp.sum((duals_new - duals_now) ** 2)
        weight_now = jnp.exp(0.25 * jnp.log((dual_move + EPSILON) / (primal_move + EPSILON)) + 0.5 * jnp.log(weight_now))
        first_now, recourse_now, duals_now = first_new, recourse_new, duals_new
    return first_now, recourse_now, duals_now, weight_now.astype(jnp.float32)
```

```python
import jax
import jax.numpy as jnp
from jax import lax
from jax.experimental import pallas as pl
from jax.experimental.pallas import tpu as pltpu
from jax.sharding import PartitionSpec as P

MESH = pl.DeviceIdType.MESH
ITERS = 4
STEP_SCALE = 0.8
EPSILON = 1e-06
SCEN, ROWS, FIRST, REC = 2, 2048, 512, 1536
COLS = FIRST + REC
WIDE = 512
TRAIL = 128


def split_rows(value):
    upper = value.astype(jnp.bfloat16).astype(jnp.float32)
    return jnp.concatenate([upper, value - upper], 0).astype(jnp.bfloat16)


def kernel(
    tech_hbm,
    rec_hbm,
    first_cost_hbm,
    rec_cost_hbm,
    demand_hbm,
    first_upper_hbm,
    rec_upper_hbm,
    first_start_hbm,
    rec_start_hbm,
    dual_start_hbm,
    first_out,
    rec_out,
    dual_out,
    weight_out,
    mat,
    mat_t,
    first_cost,
    rec_cost,
    demand,
    first_upper,
    rec_upper,
    first_now,
    rec_now,
    duals,
    sums,
    weight,
    tech_slot,
    rec_slot,
    act_slot,
    move_slot,
    load_sem,
    small_sem,
    tech_send,
    tech_recv,
    rec_send,
    rec_recv,
    act_send,
    act_recv,
    move_send,
    move_recv,
):
    scen, row, col = lax.axis_index("scen"), lax.axis_index("row"), lax.axis_index("col")
    place = scen * 4 + row

    row_peers = [{"row": lax.rem(row + d, 4)} for d in (2, 1, 3)]
    col_peers = [{"col": lax.rem(col + d, 8)} for d in (4, 5, 3, 2, 6, 1, 7)]
    block_peers = [
        {"scen": lax.rem(scen + d, 4), "row": lax.rem(row + e, 4)}
        for d in (2, 1, 3, 0)
        for e in (2, 1, 3, 0)
        if d or e
    ]

    barrier = pltpu.get_barrier_semaphore()
    for peer in block_peers + col_peers:
        pl.semaphore_signal(barrier, inc=1, device_id=peer, device_id_type=MESH)

    pieces = []
    for part in range(4):
        for s in range(SCEN):
            if part == 0:
                source = tech_hbm.at[s]
            else:
                source = rec_hbm.at[s, :, pl.ds((part - 1) * WIDE, WIDE)]
            pieces.append(
                pltpu.make_async_copy(
                    source, mat.at[s, :, pl.ds(part * WIDE, WIDE)], load_sem.at[part, s]
                )
            )
    smalls = [
        pltpu.make_async_copy(dual_start_hbm, duals, small_sem.at[0]),
        pltpu.make_async_copy(demand_hbm, demand, small_sem.at[1]),
        pltpu.make_async_copy(rec_cost_hbm, rec_cost, small_sem.at[2]),
        pltpu.make_async_copy(rec_upper_hbm, rec_upper, small_sem.at[3]),
        pltpu.make_async_copy(rec_start_hbm, rec_now, small_sem.at[4]),
        pltpu.make_async_copy(first_cost_hbm, first_cost, small_sem.at[5]),
        pltpu.make_async_copy(first_upper_hbm, first_upper, small_sem.at[6]),
        pltpu.make_async_copy(first_start_hbm, first_now, small_sem.at[7]),
    ]
    for copy in smalls[:1] + pieces + smalls[1:]:
        copy.start()

    def send(slot, mine, peers, send_sem, recv_sem):
        for peer in peers:
            pltpu.make_async_remote_copy(
                src_ref=slot.at[mine],
                dst_ref=slot.at[mine],
                send_sem=send_sem,
                recv_sem=recv_sem,
                device_id=peer,
                device_id_type=MESH,
            ).start()

    def wait_bytes(slot, count, sem):
        view = slot.at[pl.ds(0, count)]
        pltpu.make_async_copy(view, view, sem).wait()

    def back(left, s, part):
        out = jnp.dot(
            left,
            mat[s, :, pl.ds(part * WIDE, WIDE)],
            preferred_element_type=jnp.float32,
        )
        return out[s : s + 1] + out[2 + s : 3 + s]

    def back_part(left, it, part):
        if part == 0:
            total = back(left, 0, 0) + back(left, 1, 0)
            tech_slot[it, pl.ds(place, 1)] = total.reshape(1, 1, WIDE)
            send(
                tech_slot.at[it], place, block_peers, tech_send.at[it], tech_recv.at[it]
            )
        else:
            for s in range(SCEN):
                rec_slot[it, part - 1, row, pl.ds(s, 1)] = back(left, s, part)
            send(
                rec_slot.at[it, part - 1],
                row,
                row_peers,
                rec_send.at[it, part - 1],
                rec_recv.at[it, part - 1],
            )

    def turn(s, part):
        for k in range(2):
            cols = pl.ds(part * WIDE + k * 256, 256)
            mat_t[s, cols, :] = mat[s, :, cols].T

    smalls[0].wait()
    weight[...] = jnp.ones_like(weight)
    left = split_rows(duals[...])
    for part in range(4):
        pieces[part * 2].wait()
        pieces[part * 2 + 1].wait()
        if part == 0:
            pl.semaphore_wait(barrier, 22)
        back_part(left, 0, part)
        if part < 3:
            turn(0, part)
            turn(1, part)
    turn(0, 3)
    turn(1, 3)
    for copy in smalls[1:]:
        copy.wait()

    def forward(left, part):
        for s in range(SCEN):
            out = jnp.dot(
                left,
                mat_t[s, pl.ds(part * WIDE, WIDE), :],
                preferred_element_type=jnp.float32,
            )
            sums[s] = out if part == 1 else sums[s] + out

    def iterate(it, carry):
        now = weight[:, 0:1]
        step_primal = STEP_SCALE / now
        step_dual = STEP_SCALE * now
        rec_move = jnp.zeros((1, 1), jnp.float32)
        first_move = jnp.zeros((1, 1), jnp.float32)
        for part in (1, 2, 0, 3):
            if part == 0:
                wait_bytes(tech_slot.at[it], 15, tech_recv.at[it])
                grad = tech_slot[it, 0]
                for p in range(1, 16):
                    grad = grad + tech_slot[it, p]
                old = first_now[...]
                new = jnp.clip(
                    old - step_primal * (first_cost[...] - grad), 0.0, first_upper[...]
                )
                first_now[...] = new
                bar = jnp.broadcast_to(2.0 * new - old, (SCEN, FIRST))
                first_move = jnp.sum((new - old) ** 2, keepdims=True)
            else:
                wait_bytes(rec_slot.at[it, part - 1], 3, rec_recv.at[it, part - 1])
                grad = rec_slot[it, part - 1, 0]
                for p in range(1, 4):
                    grad = grad + rec_slot[it, part - 1, p]
                cols = pl.ds((part - 1) * WIDE, WIDE)
                old = rec_now[:, cols]
                new = jnp.clip(
                    old - step_primal * (rec_cost[:, cols] - grad), 0.0, rec_upper[:, cols]
                )
                rec_now[:, cols] = new
                bar = 2.0 * new - old
                rec_move = rec_move + jnp.sum((new - old) ** 2, keepdims=True)
            forward(split_rows(bar), part)
        for s in range(SCEN):
            act_slot[it, col, pl.ds(s, 1), pl.ds(0, ROWS)] = sums[s, s : s + 1] + sums[s, 2 + s : 3 + s]
        act_slot[it, col, :, pl.ds(ROWS, TRAIL)] = jnp.broadcast_to(
            0.25 * rec_move + 0.0625 * first_move, (SCEN, TRAIL)
        )
        send(act_slot.at[it], col, col_peers, act_send.at[it], act_recv.at[it])
        wait_bytes(act_slot.at[it], 7, act_recv.at[it])
        activity = act_slot[it, 0]
        for p in range(1, 8):
            activity = activity + act_slot[it, p]
        old = duals[...]
        new = jnp.maximum(0.0, old + step_dual * (demand[...] - activity[:, :ROWS]))
        duals[...] = new
        dual_move = jnp.sum((new - old) ** 2, keepdims=True)
        move_slot[it, pl.ds(place, 1)] = jnp.concatenate(
            [jnp.broadcast_to(dual_move, (1, TRAIL)), activity[0:1, ROWS:]], 0
        ).reshape(1, 2, TRAIL)
        send(move_slot.at[it], place, block_peers, move_send.at[it], move_recv.at[it])

        @pl.when(it < ITERS - 1)
        def _():
            left = split_rows(duals[...])
            for part in range(4):
                back_part(left, it + 1, part)

        wait_bytes(move_slot.at[it], 15, move_recv.at[it])
        moves = move_slot[it, 0]
        for p in range(1, 16):
            moves = moves + move_slot[it, p]
        before = weight[...]
        weight[...] = jnp.exp(
            0.25 * jnp.log((moves[0:1] + EPSILON) / (moves[1:2] + EPSILON))
            + 0.5 * jnp.log(before)
        )
        return carry

    lax.fori_loop(0, ITERS, iterate, 0)

    first_out[...] = first_now[...]
    rec_out[...] = rec_now[...]
    dual_out[...] = duals[...]
    weight_out[...] = weight[...]

    def drain(it, carry):
        wait_bytes(tech_slot.at[it], 15, tech_send.at[it])
        for part in range(3):
            wait_bytes(rec_slot.at[it, part], 3, rec_send.at[it, part])
        wait_bytes(act_slot.at[it], 7, act_send.at[it])
        wait_bytes(move_slot.at[it], 15, move_send.at[it])
        return carry

    lax.fori_loop(0, ITERS, drain, 0)


def local(
    tech_matrix,
    recourse_matrix,
    first_cost,
    recourse_cost,
    demand,
    first_upper,
    recourse_upper,
    first_start,
    recourse_start,
    dual_start,
):
    f32 = jnp.float32
    dma = pltpu.SemaphoreType.DMA
    first, rec, duals, weight = pl.pallas_call(
        kernel,
        out_shape=(
            jax.ShapeDtypeStruct((1, FIRST), f32),
            jax.ShapeDtypeStruct((SCEN, REC), f32),
            jax.ShapeDtypeStruct((SCEN, ROWS), f32),
            jax.ShapeDtypeStruct((1, TRAIL), f32),
        ),
        in_specs=[pl.BlockSpec(memory_space=pltpu.HBM)] * 10,
        out_specs=[pl.BlockSpec(memory_space=pltpu.VMEM)] * 4,
        scratch_shapes=[
            pltpu.VMEM((SCEN, ROWS, COLS), jnp.bfloat16),
            pltpu.VMEM((SCEN, COLS, ROWS), jnp.bfloat16),
            pltpu.VMEM((1, FIRST), f32),
            pltpu.VMEM((SCEN, REC), f32),
            pltpu.VMEM((SCEN, ROWS), f32),
            pltpu.VMEM((1, FIRST), f32),
            pltpu.VMEM((SCEN, REC), f32),
            pltpu.VMEM((1, FIRST), f32),
            pltpu.VMEM((SCEN, REC), f32),
            pltpu.VMEM((SCEN, ROWS), f32),
            pltpu.VMEM((SCEN, 2 * SCEN, ROWS), f32),
            pltpu.VMEM((1, TRAIL), f32),
            pltpu.VMEM((ITERS, 16, 1, FIRST), f32),
            pltpu.VMEM((ITERS, 3, 4, SCEN, WIDE), f32),
            pltpu.VMEM((ITERS, 8, SCEN, ROWS + TRAIL), f32),
            pltpu.VMEM((ITERS, 16, 2, TRAIL), f32),
            dma((4, SCEN)),
            dma((8,)),
            dma((ITERS,)),
            dma((ITERS,)),
            dma((ITERS, 3)),
            dma((ITERS, 3)),
            dma((ITERS,)),
            dma((ITERS,)),
            dma((ITERS,)),
            dma((ITERS,)),
        ],
        compiler_params=pltpu.CompilerParams(
            collective_id=0, has_side_effects=True, vmem_limit_bytes=48 * 2**20
        ),
    )(
        tech_matrix,
        recourse_matrix,
        first_cost.reshape(1, FIRST),
        recourse_cost,
        demand,
        first_upper.reshape(1, FIRST),
        recourse_upper,
        first_start.reshape(1, FIRST),
        recourse_start,
        dual_start,
    )
    return first.reshape(FIRST), rec, duals, weight[0, 0]


def solution(mesh):
    in_specs = (
        P("scen", "row", "col"),
        P("scen", "row", "col"),
        P("col"),
        P("scen", "col"),
        P("scen", "row"),
        P("col"),
        P("scen", "col"),
        P("col"),
        P("scen", "col"),
        P("scen", "row"),
    )
    out_specs = (P("col"), P("scen", "col"), P("scen", "row"), P())
    return jax.shard_map(local, mesh=mesh, in_specs=in_specs, out_specs=out_specs, check_vma=False)
```

```python
import jax
import jax.numpy as jnp
from jax import lax
from jax.experimental import pallas as pl
from jax.experimental.pallas import tpu as pltpu
from jax.sharding import PartitionSpec as P

MESH = pl.DeviceIdType.MESH
ITERS = 4
STEP_SCALE = 0.8
EPSILON = 1e-06
SCEN, ROWS, FIRST, REC = 2, 2048, 512, 1536
COLS = FIRST + REC
WIDE = 512
TRAIL = 128
EARLY = ((0, 0), (0, 1), (1, 0), (1, 1), (2, 0))


def split_rows(value):
    upper = value.astype(jnp.bfloat16).astype(jnp.float32)
    return jnp.concatenate([upper, value - upper], 0).astype(jnp.bfloat16)


def kernel(
    tech_hbm,
    rec_hbm,
    first_cost_hbm,
    rec_cost_hbm,
    demand_hbm,
    first_upper_hbm,
    rec_upper_hbm,
    first_start_hbm,
    rec_start_hbm,
    dual_start_hbm,
    first_out,
    rec_out,
    dual_out,
    weight_out,
    mat,
    mat_t,
    first_cost,
    rec_cost,
    demand,
    first_upper,
    rec_upper,
    first_now,
    rec_now,
    duals,
    sums,
    weight,
    tech_part,
    tech_slot,
    rec_slot,
    act_slot,
    move_slot,
    load_sem,
    small_sem,
    tech_send,
    tech_recv,
    rec_send,
    rec_recv,
    act_send,
    act_recv,
    move_send,
    move_recv,
):
    scen, row, col = lax.axis_index("scen"), lax.axis_index("row"), lax.axis_index("col")
    place = scen * 4 + row

    row_peers = [{"row": lax.rem(row + d, 4)} for d in (2, 1, 3)]
    col_peers = [{"col": lax.rem(col + d, 8)} for d in (4, 5, 3, 2, 6, 1, 7)]
    block_peers = [
        {"scen": lax.rem(scen + d, 4), "row": lax.rem(row + e, 4)}
        for d in (2, 1, 3, 0)
        for e in (2, 1, 3, 0)
        if d or e
    ]

    barrier = pltpu.get_barrier_semaphore()
    for peer in block_peers + col_peers:
        pl.semaphore_signal(barrier, inc=1, device_id=peer, device_id_type=MESH)

    pieces = []
    for part in range(4):
        for s in range(SCEN):
            if part == 0:
                source = tech_hbm.at[s]
            else:
                source = rec_hbm.at[s, :, pl.ds((part - 1) * WIDE, WIDE)]
            pieces.append(
                pltpu.make_async_copy(
                    source, mat.at[s, :, pl.ds(part * WIDE, WIDE)], load_sem.at[part, s]
                )
            )
    smalls = [
        pltpu.make_async_copy(dual_start_hbm, duals, small_sem.at[0]),
        pltpu.make_async_copy(demand_hbm, demand, small_sem.at[1]),
        pltpu.make_async_copy(rec_cost_hbm, rec_cost, small_sem.at[2]),
        pltpu.make_async_copy(rec_upper_hbm, rec_upper, small_sem.at[3]),
        pltpu.make_async_copy(rec_start_hbm, rec_now, small_sem.at[4]),
        pltpu.make_async_copy(first_cost_hbm, first_cost, small_sem.at[5]),
        pltpu.make_async_copy(first_upper_hbm, first_upper, small_sem.at[6]),
        pltpu.make_async_copy(first_start_hbm, first_now, small_sem.at[7]),
    ]
    for copy in smalls[:1] + pieces + smalls[1:]:
        copy.start()

    def send(slot, mine, peers, send_sem, recv_sem):
        for peer in peers:
            pltpu.make_async_remote_copy(
                src_ref=slot.at[mine],
                dst_ref=slot.at[mine],
                send_sem=send_sem,
                recv_sem=recv_sem,
                device_id=peer,
                device_id_type=MESH,
            ).start()

    def wait_bytes(slot, count, sem):
        view = slot.at[pl.ds(0, count)]
        pltpu.make_async_copy(view, view, sem).wait()

    def back(left, s, part):
        out = jnp.dot(
            left,
            mat[s, :, pl.ds(part * WIDE, WIDE)],
            preferred_element_type=jnp.float32,
        )
        return out[0:1] + out[1:2]

    def send_tech(it, total):
        tech_slot[it, pl.ds(place, 1)] = total.reshape(1, 1, WIDE)
        send(tech_slot.at[it], place, block_peers, tech_send.at[it], tech_recv.at[it])

    def send_rec(it, part):
        send(
            rec_slot.at[it, part - 1],
            row,
            row_peers,
            rec_send.at[it, part - 1],
            rec_recv.at[it, part - 1],
        )

    def turn(s, part):
        for k in range(2):
            cols = pl.ds(part * WIDE + k * 256, 256)
            mat_t[s, cols, :] = mat[s, :, cols].T

    smalls[0].wait()
    weight[...] = jnp.ones_like(weight)
    left = [split_rows(duals[s : s + 1, :]) for s in range(SCEN)]
    total = None
    for part in range(4):
        for s in range(SCEN):
            pieces[part * 2 + s].wait()
            out = back(left[s], s, part)
            if part == 0:
                total = out if s == 0 else total + out
            else:
                rec_slot[0, part - 1, row, pl.ds(s, 1)] = out
            if (part, s) in EARLY:
                turn(s, part)
        if part == 0:
            pl.semaphore_wait(barrier, 22)
            send_tech(0, total)
        else:
            send_rec(0, part)
    for part in (1, 2, 0, 3):
        for s in range(SCEN):
            if (part, s) not in EARLY:
                turn(s, part)
    for copy in smalls[1:]:
        copy.wait()

    def forward(left, s, part):
        return jnp.dot(
            left,
            mat_t[s, pl.ds(part * WIDE, WIDE), :],
            preferred_element_type=jnp.float32,
        )

    def iterate(it, carry):
        now = weight[:, 0:1]
        step_primal = STEP_SCALE / now
        step_dual = STEP_SCALE * now
        move = jnp.zeros((1, WIDE), jnp.float32)
        for part in (1, 2, 0, 3):
            if part == 0:
                wait_bytes(tech_slot.at[it], 15, tech_recv.at[it])
                grad = tech_slot[it, 0]
                for p in range(1, 16):
                    grad = grad + tech_slot[it, p]
                old = first_now[...]
                new = jnp.clip(
                    old - step_primal * (first_cost[...] - grad), 0.0, first_upper[...]
                )
                first_now[...] = new
                bar = jnp.broadcast_to(2.0 * new - old, (SCEN, FIRST))
                move = move + 0.0625 * (new - old) ** 2
            else:
                wait_bytes(rec_slot.at[it, part - 1], 3, rec_recv.at[it, part - 1])
                grad = rec_slot[it, part - 1, 0]
                for p in range(1, 4):
                    grad = grad + rec_slot[it, part - 1, p]
                cols = pl.ds((part - 1) * WIDE, WIDE)
                old = rec_now[:, cols]
                new = jnp.clip(
                    old - step_primal * (rec_cost[:, cols] - grad), 0.0, rec_upper[:, cols]
                )
                rec_now[:, cols] = new
                bar = 2.0 * new - old
                square = 0.25 * (new - old) ** 2
                move = move + square[0:1] + square[1:2]
            left = split_rows(bar)
            if part == 3:
                spread = move[:, 0:TRAIL]
                for k in range(1, WIDE // TRAIL):
                    spread = spread + move[:, k * TRAIL : (k + 1) * TRAIL]
                for s in range(SCEN):
                    act_slot[it, s, col, :, pl.ds(ROWS, TRAIL)] = spread
            for s in range(SCEN):
                out = forward(left, s, part)
                if part == 1:
                    sums[s] = out
                elif part != 3:
                    sums[s] = sums[s] + out
                else:
                    out = sums[s] + out
                    act_slot[it, s, col, :, pl.ds(0, ROWS)] = out[s : s + 1] + out[2 + s : 3 + s]
                    send(
                        act_slot.at[it, s], col, col_peers, act_send.at[it, s], act_recv.at[it, s]
                    )

        def dual_step(s):
            wait_bytes(act_slot.at[it, s], 7, act_recv.at[it, s])
            activity = act_slot[it, s, 0]
            for p in range(1, 8):
                activity = activity + act_slot[it, s, p]
            old = duals[s : s + 1, :]
            new = jnp.maximum(
                0.0, old + step_dual * (demand[s : s + 1, :] - activity[:, :ROWS])
            )
            duals[s : s + 1, :] = new
            square = (new - old) ** 2
            spread = square[:, 0:TRAIL]
            for k in range(1, ROWS // TRAIL):
                spread = spread + square[:, k * TRAIL : (k + 1) * TRAIL]
            return new, spread, activity[:, ROWS:]

        new_0, spread_0, _ = dual_step(0)
        left_0 = split_rows(new_0)
        tech_part[...] = back(left_0, 0, 0)
        new_1, spread_1, primal = dual_step(1)
        move_slot[it, pl.ds(place, 1)] = jnp.concatenate([spread_0 + spread_1, primal], 0).reshape(
            1, 2, TRAIL
        )
        send(move_slot.at[it], place, block_peers, move_send.at[it], move_recv.at[it])

        @pl.when(it < ITERS - 1)
        def _():
            left = [split_rows(duals[s : s + 1, :]) for s in range(SCEN)]
            send_tech(it + 1, tech_part[...] + back(left[1], 1, 0))
            for part in (1, 2, 3):
                for s in range(SCEN):
                    rec_slot[it + 1, part - 1, row, pl.ds(s, 1)] = back(left[s], s, part)
                send_rec(it + 1, part)

        wait_bytes(move_slot.at[it], 15, move_recv.at[it])
        moves = move_slot[it, 0]
        for p in range(1, 16):
            moves = moves + move_slot[it, p]
        moves = jnp.sum(moves, 1, keepdims=True) + EPSILON
        before = weight[...]
        weight[...] = jnp.exp(0.25 * jnp.log(moves[0:1] / moves[1:2]) + 0.5 * jnp.log(before))
        return carry

    lax.fori_loop(0, ITERS, iterate, 0)

    first_out[...] = first_now[...]
    rec_out[...] = rec_now[...]
    dual_out[...] = duals[...]
    weight_out[...] = weight[:, 0:1]

    def drain(it, carry):
        wait_bytes(tech_slot.at[it], 15, tech_send.at[it])
        for part in range(3):
            wait_bytes(rec_slot.at[it, part], 3, rec_send.at[it, part])
        for s in range(SCEN):
            wait_bytes(act_slot.at[it, s], 7, act_send.at[it, s])
        wait_bytes(move_slot.at[it], 15, move_send.at[it])
        return carry

    lax.fori_loop(0, ITERS, drain, 0)


def place_outputs(first, rec, duals, weight, first_out, rec_out, dual_out, weight_out, sem):
    copies = [
        pltpu.make_async_copy(first, first_out, sem.at[0]),
        pltpu.make_async_copy(rec, rec_out, sem.at[1]),
        pltpu.make_async_copy(duals, dual_out, sem.at[2]),
        pltpu.make_async_copy(weight, weight_out, sem.at[3]),
    ]
    for copy in copies:
        copy.start()
    for copy in copies:
        copy.wait()


def local(
    tech_matrix,
    recourse_matrix,
    first_cost,
    recourse_cost,
    demand,
    first_upper,
    recourse_upper,
    first_start,
    recourse_start,
    dual_start,
):
    f32 = jnp.float32
    dma = pltpu.SemaphoreType.DMA
    first, rec, duals, weight = pl.pallas_call(
        kernel,
        out_shape=(
            jax.ShapeDtypeStruct((1, FIRST), f32),
            jax.ShapeDtypeStruct((SCEN, REC), f32),
            jax.ShapeDtypeStruct((SCEN, ROWS), f32),
            jax.ShapeDtypeStruct((1, 1), f32),
        ),
        in_specs=[pl.BlockSpec(memory_space=pltpu.HBM)] * 10,
        out_specs=[pl.BlockSpec(memory_space=pltpu.VMEM)] * 4,
        scratch_shapes=[
            pltpu.VMEM((SCEN, ROWS, COLS), jnp.bfloat16),
            pltpu.VMEM((SCEN, COLS, ROWS), jnp.bfloat16),
            pltpu.VMEM((1, FIRST), f32),
            pltpu.VMEM((SCEN, REC), f32),
            pltpu.VMEM((SCEN, ROWS), f32),
            pltpu.VMEM((1, FIRST), f32),
            pltpu.VMEM((SCEN, REC), f32),
            pltpu.VMEM((1, FIRST), f32),
            pltpu.VMEM((SCEN, REC), f32),
            pltpu.VMEM((SCEN, ROWS), f32),
            pltpu.VMEM((SCEN, 2 * SCEN, ROWS), f32),
            pltpu.VMEM((1, TRAIL), f32),
            pltpu.VMEM((1, FIRST), f32),
            pltpu.VMEM((ITERS, 16, 1, FIRST), f32),
            pltpu.VMEM((ITERS, 3, 4, SCEN, WIDE), f32),
            pltpu.VMEM((ITERS, SCEN, 8, 1, ROWS + TRAIL), f32),
            pltpu.VMEM((ITERS, 16, 2, TRAIL), f32),
            dma((4, SCEN)),
            dma((8,)),
            dma((ITERS,)),
            dma((ITERS,)),
            dma((ITERS, 3)),
            dma((ITERS, 3)),
            dma((ITERS, SCEN)),
            dma((ITERS, SCEN)),
            dma((ITERS,)),
            dma((ITERS,)),
        ],
        compiler_params=pltpu.CompilerParams(
            collective_id=0, has_side_effects=True, vmem_limit_bytes=63 * 2**20
        ),
    )(
        tech_matrix,
        recourse_matrix,
        first_cost.reshape(1, FIRST),
        recourse_cost,
        demand,
        first_upper.reshape(1, FIRST),
        recourse_upper,
        first_start.reshape(1, FIRST),
        recourse_start,
        dual_start,
    )
    outs = pl.pallas_call(
        place_outputs,
        out_shape=(
            jax.ShapeDtypeStruct((1, FIRST), f32),
            jax.ShapeDtypeStruct((SCEN, REC), f32),
            jax.ShapeDtypeStruct((SCEN, ROWS), f32),
            jax.ShapeDtypeStruct((1, 1), f32),
        ),
        in_specs=[pl.BlockSpec(memory_space=pl.ANY)] * 4,
        out_specs=[pl.BlockSpec(memory_space=pltpu.HBM)] * 4,
        scratch_shapes=[dma((4,))],
        compiler_params=pltpu.CompilerParams(vmem_limit_bytes=63 * 2**20),
    )(first, rec, duals, weight)
    return outs[0].reshape(FIRST), outs[1], outs[2], outs[3].reshape(())


def solution(mesh):
    in_specs = (
        P("scen", "row", "col"),
        P("scen", "row", "col"),
        P("col"),
        P("scen", "col"),
        P("scen", "row"),
        P("col"),
        P("scen", "col"),
        P("col"),
        P("scen", "col"),
        P("scen", "row"),
    )
    out_specs = (P("col"), P("scen", "col"), P("scen", "row"), P())
    return jax.shard_map(local, mesh=mesh, in_specs=in_specs, out_specs=out_specs, check_vma=False)
```

```python
import jax
import jax.numpy as jnp
from jax import lax
from jax.experimental import pallas as pl
from jax.experimental.pallas import tpu as pltpu
from jax.sharding import PartitionSpec as P

MESH = pl.DeviceIdType.MESH
ITERS = 4
STEP_SCALE = 0.8
EPSILON = 1e-06
SCEN, ROWS, FIRST, REC = 2, 2048, 512, 1536
COLS = FIRST + REC
WIDE = 512
PLACE = (2, 0, 1, 3)
TRAIL = 128
EARLY = ((0, 0), (0, 1), (1, 0), (1, 1), (2, 0))


def split_rows(value):
    upper = value.astype(jnp.bfloat16).astype(jnp.float32)
    return jnp.concatenate([upper, value - upper], 0).astype(jnp.bfloat16)


def kernel(
    tech_hbm,
    rec_hbm,
    first_cost_hbm,
    rec_cost_hbm,
    demand_hbm,
    first_upper_hbm,
    rec_upper_hbm,
    first_start_hbm,
    rec_start_hbm,
    dual_start_hbm,
    first_now,
    rec_now,
    duals,
    weight_out,
    mat,
    mat_t,
    first_cost,
    rec_cost,
    demand,
    first_upper,
    rec_upper,
    sums,
    weight,
    tech_part,
    tech_slot,
    rec_slot,
    act_slot,
    move_slot,
    load_sem,
    small_sem,
    tech_send,
    tech_recv,
    rec_send,
    rec_recv,
    act_send,
    act_recv,
    move_send,
    move_recv,
):
    scen, row, col = lax.axis_index("scen"), lax.axis_index("row"), lax.axis_index("col")
    place = scen * 4 + row

    row_peers = [{"row": lax.rem(row + d, 4)} for d in (2, 1, 3)]
    col_peers = [{"col": lax.rem(col + d, 8)} for d in (4, 5, 3, 2, 6, 1, 7)]
    block_peers = [
        {"scen": lax.rem(scen + d, 4), "row": lax.rem(row + e, 4)}
        for d in (2, 1, 3, 0)
        for e in (2, 1, 3, 0)
        if d or e
    ]

    barrier = pltpu.get_barrier_semaphore()
    for peer in block_peers + col_peers:
        pl.semaphore_signal(barrier, inc=1, device_id=peer, device_id_type=MESH)

    pieces = []
    for part in range(4):
        for s in range(SCEN):
            if part == 0:
                source = tech_hbm.at[s]
            else:
                source = rec_hbm.at[s, :, pl.ds((part - 1) * WIDE, WIDE)]
            pieces.append(
                pltpu.make_async_copy(
                    source, mat.at[s, :, pl.ds(PLACE[part] * WIDE, WIDE)], load_sem.at[part, s]
                )
            )
    smalls = [
        pltpu.make_async_copy(dual_start_hbm, duals, small_sem.at[0]),
        pltpu.make_async_copy(demand_hbm, demand, small_sem.at[1]),
        pltpu.make_async_copy(rec_cost_hbm, rec_cost, small_sem.at[2]),
        pltpu.make_async_copy(rec_upper_hbm, rec_upper, small_sem.at[3]),
        pltpu.make_async_copy(rec_start_hbm, rec_now, small_sem.at[4]),
        pltpu.make_async_copy(first_cost_hbm, first_cost, small_sem.at[5]),
        pltpu.make_async_copy(first_upper_hbm, first_upper, small_sem.at[6]),
        pltpu.make_async_copy(first_start_hbm, first_now, small_sem.at[7]),
    ]
    for copy in smalls[:1] + pieces + smalls[1:]:
        copy.start()

    def send(slot, mine, peers, send_sem, recv_sem):
        for peer in peers:
            pltpu.make_async_remote_copy(
                src_ref=slot.at[mine],
                dst_ref=slot.at[mine],
                send_sem=send_sem,
                recv_sem=recv_sem,
                device_id=peer,
                device_id_type=MESH,
            ).start()

    def wait_bytes(slot, count, sem):
        view = slot.at[pl.ds(0, count)]
        pltpu.make_async_copy(view, view, sem).wait()

    def back(left, s, part):
        out = jnp.dot(
            left,
            mat[s, :, pl.ds(PLACE[part] * WIDE, WIDE)],
            preferred_element_type=jnp.float32,
        )
        return out[0:1] + out[1:2]

    def send_tech(it, total):
        tech_slot[it, pl.ds(place, 1)] = total.reshape(1, 1, WIDE)
        send(tech_slot.at[it], place, block_peers, tech_send.at[it], tech_recv.at[it])

    def send_rec(it, part):
        send(
            rec_slot.at[it, part - 1],
            row,
            row_peers,
            rec_send.at[it, part - 1],
            rec_recv.at[it, part - 1],
        )

    def turn(s, part):
        for k in range(2):
            cols = pl.ds(PLACE[part] * WIDE + k * 256, 256)
            mat_t[s, cols, :] = mat[s, :, cols].T

    smalls[0].wait()
    weight[...] = jnp.zeros_like(weight)
    left = [split_rows(duals[s : s + 1, :]) for s in range(SCEN)]
    total = None
    for part in range(4):
        for s in range(SCEN):
            pieces[part * 2 + s].wait()
            out = back(left[s], s, part)
            if part == 0:
                total = out if s == 0 else total + out
            else:
                rec_slot[0, part - 1, row, pl.ds(s, 1)] = out
            if (part, s) in EARLY:
                turn(s, part)
        if part == 0:
            pl.semaphore_wait(barrier, 22)
            send_tech(0, total)
        else:
            send_rec(0, part)
    for part in (1, 2, 0, 3):
        for s in range(SCEN):
            if (part, s) not in EARLY:
                turn(s, part)
    for copy in smalls[1:]:
        copy.wait()

    def forward(bar, s, first, count):
        return jnp.dot(
            split_rows(bar),
            mat_t[s, pl.ds(first * WIDE, count * WIDE), :],
            preferred_element_type=jnp.float32,
        )

    def wide(value, count):
        return jnp.concatenate([value] * (count // TRAIL), 1)

    def iterate(it, carry):
        log_weight = weight[...]
        step_primal = wide(STEP_SCALE * jnp.exp(-log_weight), WIDE)
        step_dual = wide(STEP_SCALE * jnp.exp(log_weight), ROWS)

        def rec_step(part):
            wait_bytes(rec_slot.at[it, part - 1], 3, rec_recv.at[it, part - 1])
            grad = rec_slot[it, part - 1, 0]
            for p in range(1, 4):
                grad = grad + rec_slot[it, part - 1, p]
            cols = pl.ds((part - 1) * WIDE, WIDE)
            old = rec_now[:, cols]
            new = jnp.clip(
                old - step_primal * (rec_cost[:, cols] - grad), 0.0, rec_upper[:, cols]
            )
            rec_now[:, cols] = new
            square = 0.25 * (new - old) ** 2
            return 2.0 * new - old, square[0:1] + square[1:2]

        def first_step():
            wait_bytes(tech_slot.at[it], 15, tech_recv.at[it])
            grad = tech_slot[it, 0]
            for p in range(1, 16):
                grad = grad + tech_slot[it, p]
            old = first_now[...]
            new = jnp.clip(old - step_primal * (first_cost[...] - grad), 0.0, first_upper[...])
            first_now[...] = new
            return jnp.broadcast_to(2.0 * new - old, (SCEN, FIRST)), 0.0625 * (new - old) ** 2

        bar, move = rec_step(1)
        for s in range(SCEN):
            sums[s] = forward(bar, s, 0, 1)
        bar_2, move_2 = rec_step(2)
        bar_0, move_0 = first_step()
        bar = jnp.concatenate([bar_2, bar_0], 1)
        move = move + move_2 + move_0
        for s in range(SCEN):
            sums[s] = sums[s] + forward(bar, s, 1, 2)
        bar, move_3 = rec_step(3)
        move = move + move_3
        spread = move[:, 0:TRAIL]
        for k in range(1, WIDE // TRAIL):
            spread = spread + move[:, k * TRAIL : (k + 1) * TRAIL]
        for s in range(SCEN):
            act_slot[it, s, col, :, pl.ds(ROWS, TRAIL)] = spread
            out = sums[s] + forward(bar, s, 3, 1)
            act_slot[it, s, col, :, pl.ds(0, ROWS)] = out[s : s + 1] + out[2 + s : 3 + s]
            send(act_slot.at[it, s], col, col_peers, act_send.at[it, s], act_recv.at[it, s])

        def dual_step(s):
            wait_bytes(act_slot.at[it, s], 7, act_recv.at[it, s])
            activity = act_slot[it, s, 0]
            for p in range(1, 8):
                activity = activity + act_slot[it, s, p]
            old = duals[s : s + 1, :]
            new = jnp.maximum(
                0.0, old + step_dual * (demand[s : s + 1, :] - activity[:, :ROWS])
            )
            duals[s : s + 1, :] = new
            square = (new - old) ** 2
            spread = square[:, 0:TRAIL]
            for k in range(1, ROWS // TRAIL):
                spread = spread + square[:, k * TRAIL : (k + 1) * TRAIL]
            return new, spread, activity[:, ROWS:]

        new_0, spread_0, _ = dual_step(0)
        left_0 = split_rows(new_0)
        tech_part[...] = back(left_0, 0, 0)
        new_1, spread_1, primal = dual_step(1)
        move_slot[it, pl.ds(place, 1)] = jnp.concatenate([spread_0 + spread_1, primal], 0).reshape(
            1, 2, TRAIL
        )
        send(move_slot.at[it], place, block_peers, move_send.at[it], move_recv.at[it])

        @pl.when(it < ITERS - 1)
        def _():
            left = [split_rows(duals[s : s + 1, :]) for s in range(SCEN)]
            send_tech(it + 1, tech_part[...] + back(left[1], 1, 0))
            for part in (1, 2, 3):
                for s in range(SCEN):
                    rec_slot[it + 1, part - 1, row, pl.ds(s, 1)] = back(left[s], s, part)
                send_rec(it + 1, part)

        wait_bytes(move_slot.at[it], 15, move_recv.at[it])
        moves = move_slot[it, 0]
        for p in range(1, 16):
            moves = moves + move_slot[it, p]
        logs = jnp.log(jnp.broadcast_to(jnp.sum(moves, 1, keepdims=True), (2, TRAIL)) + EPSILON)
        weight[...] = 0.25 * (logs[0:1] - logs[1:2]) + 0.5 * log_weight
        return carry

    lax.fori_loop(0, ITERS, iterate, 0)

    weight_out[...] = jnp.exp(weight[:, 0:1])

    def drain(it, carry):
        wait_bytes(tech_slot.at[it], 15, tech_send.at[it])
        for part in range(3):
            wait_bytes(rec_slot.at[it, part], 3, rec_send.at[it, part])
        for s in range(SCEN):
            wait_bytes(act_slot.at[it, s], 7, act_send.at[it, s])
        wait_bytes(move_slot.at[it], 15, move_send.at[it])
        return carry

    lax.fori_loop(0, ITERS, drain, 0)


def place_outputs(first, rec, duals, weight, first_out, rec_out, dual_out, weight_out, sem):
    copies = [
        pltpu.make_async_copy(first, first_out, sem.at[0]),
        pltpu.make_async_copy(rec, rec_out, sem.at[1]),
        pltpu.make_async_copy(duals, dual_out, sem.at[2]),
        pltpu.make_async_copy(weight, weight_out, sem.at[3]),
    ]
    for copy in copies:
        copy.start()
    for copy in copies:
        copy.wait()


def local(
    tech_matrix,
    recourse_matrix,
    first_cost,
    recourse_cost,
    demand,
    first_upper,
    recourse_upper,
    first_start,
    recourse_start,
    dual_start,
):
    f32 = jnp.float32
    dma = pltpu.SemaphoreType.DMA
    first, rec, duals, weight = pl.pallas_call(
        kernel,
        out_shape=(
            jax.ShapeDtypeStruct((1, FIRST), f32),
            jax.ShapeDtypeStruct((SCEN, REC), f32),
            jax.ShapeDtypeStruct((SCEN, ROWS), f32),
            jax.ShapeDtypeStruct((1, 1), f32),
        ),
        in_specs=[pl.BlockSpec(memory_space=pltpu.HBM)] * 10,
        out_specs=[pl.BlockSpec(memory_space=pltpu.VMEM)] * 4,
        scratch_shapes=[
            pltpu.VMEM((SCEN, ROWS, COLS), jnp.bfloat16),
            pltpu.VMEM((SCEN, COLS, ROWS), jnp.bfloat16),
            pltpu.VMEM((1, FIRST), f32),
            pltpu.VMEM((SCEN, REC), f32),
            pltpu.VMEM((SCEN, ROWS), f32),
            pltpu.VMEM((1, FIRST), f32),
            pltpu.VMEM((SCEN, REC), f32),
            pltpu.VMEM((SCEN, 2 * SCEN, ROWS), f32),
            pltpu.VMEM((1, TRAIL), f32),
            pltpu.VMEM((1, FIRST), f32),
            pltpu.VMEM((ITERS, 16, 1, FIRST), f32),
            pltpu.VMEM((ITERS, 3, 4, SCEN, WIDE), f32),
            pltpu.VMEM((ITERS, SCEN, 8, 1, ROWS + TRAIL), f32),
            pltpu.VMEM((ITERS, 16, 2, TRAIL), f32),
            dma((4, SCEN)),
            dma((8,)),
            dma((ITERS,)),
            dma((ITERS,)),
            dma((ITERS, 3)),
            dma((ITERS, 3)),
            dma((ITERS, SCEN)),
            dma((ITERS, SCEN)),
            dma((ITERS,)),
            dma((ITERS,)),
        ],
        compiler_params=pltpu.CompilerParams(
            collective_id=0, has_side_effects=True, vmem_limit_bytes=44 * 2**20
        ),
    )(
        *(
            pltpu.with_memory_space_constraint(array, pltpu.HBM)
            for array in (
                tech_matrix,
                recourse_matrix,
                first_cost.reshape(1, FIRST),
                recourse_cost,
                demand,
                first_upper.reshape(1, FIRST),
                recourse_upper,
                first_start.reshape(1, FIRST),
                recourse_start,
                dual_start,
            )
        )
    )
    outs = pl.pallas_call(
        place_outputs,
        out_shape=(
            jax.ShapeDtypeStruct((1, FIRST), f32),
            jax.ShapeDtypeStruct((SCEN, REC), f32),
            jax.ShapeDtypeStruct((SCEN, ROWS), f32),
            jax.ShapeDtypeStruct((1, 1), f32),
        ),
        in_specs=[pl.BlockSpec(memory_space=pl.ANY)] * 4,
        out_specs=[pl.BlockSpec(memory_space=pltpu.HBM)] * 4,
        scratch_shapes=[dma((4,))],
        compiler_params=pltpu.CompilerParams(vmem_limit_bytes=1 * 2**20),
    )(first, rec, duals, weight)
    return outs[0].reshape(FIRST), outs[1], outs[2], outs[3].reshape(())


def solution(mesh):
    in_specs = (
        P("scen", "row", "col"),
        P("scen", "row", "col"),
        P("col"),
        P("scen", "col"),
        P("scen", "row"),
        P("col"),
        P("scen", "col"),
        P("col"),
        P("scen", "col"),
        P("scen", "row"),
    )
    out_specs = (P("col"), P("scen", "col"), P("scen", "row"), P())
    return jax.shard_map(local, mesh=mesh, in_specs=in_specs, out_specs=out_specs, check_vma=False)
```

```python
import jax
import jax.numpy as jnp
from jax import lax
from jax.experimental import pallas as pl
from jax.experimental.pallas import tpu as pltpu
from jax.sharding import PartitionSpec as P

MESH = pl.DeviceIdType.MESH
ITERS = 4
STEP_SCALE = 0.8
EPSILON = 1e-06
SCEN, ROWS, FIRST, REC = 2, 2048, 512, 1536
COLS = FIRST + REC
WIDE = 512
PLACE = (2, 0, 1, 3)
TRAIL = 128
EARLY = ((0, 0), (0, 1), (1, 0), (1, 1), (2, 0))


def split_rows(value):
    upper = value.astype(jnp.bfloat16).astype(jnp.float32)
    return jnp.concatenate([upper, value - upper], 0).astype(jnp.bfloat16)


def kernel(
    tech_hbm,
    rec_hbm,
    first_cost_hbm,
    rec_cost_hbm,
    demand_hbm,
    first_upper_hbm,
    rec_upper_hbm,
    first_start_hbm,
    rec_start_hbm,
    dual_start_hbm,
    first_now,
    rec_now,
    duals,
    weight_out,
    mat,
    mat_t,
    first_cost,
    rec_cost,
    demand,
    first_upper,
    rec_upper,
    sums,
    weight,
    slope,
    tech_part,
    tech_slot,
    rec_slot,
    act_slot,
    move_slot,
    load_sem,
    small_sem,
    tech_send,
    tech_recv,
    rec_send,
    rec_recv,
    act_send,
    act_recv,
    move_send,
    move_recv,
):
    scen, row, col = lax.axis_index("scen"), lax.axis_index("row"), lax.axis_index("col")
    place = scen * 4 + row

    row_peers = [{"row": lax.rem(row + d, 4)} for d in (2, 1, 3)]
    col_peers = [{"col": lax.rem(col + d, 8)} for d in (4, 5, 3, 2, 6, 1, 7)]
    block_peers = [
        {"scen": lax.rem(scen + d, 4), "row": lax.rem(row + e, 4)}
        for d in (2, 1, 3, 0)
        for e in (2, 1, 3, 0)
        if d or e
    ]

    barrier = pltpu.get_barrier_semaphore()
    for peer in block_peers + col_peers:
        pl.semaphore_signal(barrier, inc=1, device_id=peer, device_id_type=MESH)

    pieces = []
    for part in range(4):
        for s in range(SCEN):
            if part == 0:
                source = tech_hbm.at[s]
            else:
                source = rec_hbm.at[s, :, pl.ds((part - 1) * WIDE, WIDE)]
            pieces.append(
                pltpu.make_async_copy(
                    source, mat.at[s, :, pl.ds(PLACE[part] * WIDE, WIDE)], load_sem.at[part, s]
                )
            )
    smalls = [
        pltpu.make_async_copy(dual_start_hbm, duals, small_sem.at[0]),
        pltpu.make_async_copy(demand_hbm, demand, small_sem.at[1]),
        pltpu.make_async_copy(rec_cost_hbm, rec_cost, small_sem.at[2]),
        pltpu.make_async_copy(rec_upper_hbm, rec_upper, small_sem.at[3]),
        pltpu.make_async_copy(rec_start_hbm, rec_now, small_sem.at[4]),
        pltpu.make_async_copy(first_cost_hbm, first_cost, small_sem.at[5]),
        pltpu.make_async_copy(first_upper_hbm, first_upper, small_sem.at[6]),
        pltpu.make_async_copy(first_start_hbm, first_now, small_sem.at[7]),
    ]
    for copy in smalls[:1] + pieces + smalls[1:]:
        copy.start()

    def send(slot, mine, peers, send_sem, recv_sem):
        for peer in peers:
            pltpu.make_async_remote_copy(
                src_ref=slot.at[mine],
                dst_ref=slot.at[mine],
                send_sem=send_sem,
                recv_sem=recv_sem,
                device_id=peer,
                device_id_type=MESH,
            ).start()

    def wait_bytes(slot, count, sem):
        view = slot.at[pl.ds(0, count)]
        pltpu.make_async_copy(view, view, sem).wait()

    def back(left, s, part):
        out = jnp.dot(
            left,
            mat[s, :, pl.ds(PLACE[part] * WIDE, WIDE)],
            preferred_element_type=jnp.float32,
        )
        return out[0:1] + out[1:2]

    def send_tech(it, total):
        tech_slot[it, pl.ds(place, 1)] = total.reshape(1, 1, WIDE)
        send(tech_slot.at[it], place, block_peers, tech_send.at[it], tech_recv.at[it])

    def send_rec(it, part):
        send(
            rec_slot.at[it, part - 1],
            row,
            row_peers,
            rec_send.at[it, part - 1],
            rec_recv.at[it, part - 1],
        )

    def turn(s, part):
        for k in range(2):
            cols = pl.ds(PLACE[part] * WIDE + k * 256, 256)
            mat_t[s, cols, :] = mat[s, :, cols].T

    smalls[0].wait()
    weight[...] = jnp.zeros_like(weight)
    left = [split_rows(duals[s : s + 1, :]) for s in range(SCEN)]
    total = None
    for part in range(4):
        for s in range(SCEN):
            pieces[part * 2 + s].wait()
            out = back(left[s], s, part)
            if part == 0:
                total = out if s == 0 else total + out
            else:
                rec_slot[0, part - 1, row, pl.ds(s, 1)] = out
            if (part, s) in EARLY:
                turn(s, part)
        if part == 0:
            pl.semaphore_wait(barrier, 22)
            send_tech(0, total)
        else:
            send_rec(0, part)
    for part in (1, 2, 0, 3):
        for s in range(SCEN):
            if (part, s) not in EARLY:
                turn(s, part)
    for copy in smalls[1:]:
        copy.wait()

    def forward(bar, s, first, count):
        return jnp.dot(
            split_rows(bar),
            mat_t[s, pl.ds(first * WIDE, count * WIDE), :],
            preferred_element_type=jnp.float32,
        )

    def wide(value, count):
        return jnp.concatenate([value] * (count // TRAIL), 1)

    def rec_slope(it, part):
        wait_bytes(rec_slot.at[it, part - 1], 3, rec_recv.at[it, part - 1])
        grad = rec_slot[it, part - 1, 0]
        for p in range(1, 4):
            grad = grad + rec_slot[it, part - 1, p]
        return rec_cost[:, pl.ds((part - 1) * WIDE, WIDE)] - grad

    slope[...] = rec_slope(0, 1)

    def iterate(it, carry):
        log_weight = weight[...]
        step_primal = wide(STEP_SCALE * jnp.exp(-log_weight), WIDE)
        step_dual = wide(STEP_SCALE * jnp.exp(log_weight), ROWS)

        def rec_step(part):
            cols = pl.ds((part - 1) * WIDE, WIDE)
            old = rec_now[:, cols]
            fall = slope[...] if part == 1 else rec_slope(it, part)
            new = jnp.clip(old - step_primal * fall, 0.0, rec_upper[:, cols])
            rec_now[:, cols] = new
            square = 0.25 * (new - old) ** 2
            return 2.0 * new - old, square[0:1] + square[1:2]

        def first_step():
            wait_bytes(tech_slot.at[it], 15, tech_recv.at[it])
            grad = tech_slot[it, 0]
            for p in range(1, 16):
                grad = grad + tech_slot[it, p]
            old = first_now[...]
            new = jnp.clip(old - step_primal * (first_cost[...] - grad), 0.0, first_upper[...])
            first_now[...] = new
            return jnp.broadcast_to(2.0 * new - old, (SCEN, FIRST)), 0.0625 * (new - old) ** 2

        bar, move = rec_step(1)
        for s in range(SCEN):
            sums[s] = forward(bar, s, 0, 1)
        bar_2, move_2 = rec_step(2)
        bar_0, move_0 = first_step()
        bar = jnp.concatenate([bar_2, bar_0], 1)
        move = move + move_2 + move_0
        for s in range(SCEN):
            sums[s] = sums[s] + forward(bar, s, 1, 2)
        bar, move_3 = rec_step(3)
        move = move + move_3
        spread = move[:, 0:TRAIL]
        for k in range(1, WIDE // TRAIL):
            spread = spread + move[:, k * TRAIL : (k + 1) * TRAIL]
        for s in range(SCEN):
            act_slot[it, s, col, :, pl.ds(ROWS, TRAIL)] = spread
            out = sums[s] + forward(bar, s, 3, 1)
            act_slot[it, s, col, :, pl.ds(0, ROWS)] = out[s : s + 1] + out[2 + s : 3 + s]
            send(act_slot.at[it, s], col, col_peers, act_send.at[it, s], act_recv.at[it, s])

        def dual_step(s):
            wait_bytes(act_slot.at[it, s], 7, act_recv.at[it, s])
            activity = act_slot[it, s, 0]
            for p in range(1, 8):
                activity = activity + act_slot[it, s, p]
            old = duals[s : s + 1, :]
            new = jnp.maximum(
                0.0, old + step_dual * (demand[s : s + 1, :] - activity[:, :ROWS])
            )
            duals[s : s + 1, :] = new
            square = (new - old) ** 2
            spread = square[:, 0:TRAIL]
            for k in range(1, ROWS // TRAIL):
                spread = spread + square[:, k * TRAIL : (k + 1) * TRAIL]
            return new, spread, activity[:, ROWS:]

        new_0, spread_0, _ = dual_step(0)
        left_0 = split_rows(new_0)
        tech_part[...] = back(left_0, 0, 0)
        new_1, spread_1, primal = dual_step(1)
        move_slot[it, pl.ds(place, 1)] = jnp.concatenate([spread_0 + spread_1, primal], 0).reshape(
            1, 2, TRAIL
        )
        send(move_slot.at[it], place, block_peers, move_send.at[it], move_recv.at[it])

        @pl.when(it < ITERS - 1)
        def _():
            left = [split_rows(duals[s : s + 1, :]) for s in range(SCEN)]
            send_tech(it + 1, tech_part[...] + back(left[1], 1, 0))
            for part in (1, 2, 3):
                for s in range(SCEN):
                    rec_slot[it + 1, part - 1, row, pl.ds(s, 1)] = back(left[s], s, part)
                send_rec(it + 1, part)
            slope[...] = rec_slope(it + 1, 1)

        wait_bytes(move_slot.at[it], 15, move_recv.at[it])
        moves = move_slot[it, 0]
        for p in range(1, 16):
            moves = moves + move_slot[it, p]
        logs = jnp.log(jnp.broadcast_to(jnp.sum(moves, 1, keepdims=True), (2, TRAIL)) + EPSILON)
        weight[...] = 0.25 * (logs[0:1] - logs[1:2]) + 0.5 * log_weight
        return carry

    lax.fori_loop(0, ITERS, iterate, 0)

    weight_out[...] = jnp.exp(weight[:, 0:1])

    def drain(it, carry):
        wait_bytes(tech_slot.at[it], 15, tech_send.at[it])
        for part in range(3):
            wait_bytes(rec_slot.at[it, part], 3, rec_send.at[it, part])
        for s in range(SCEN):
            wait_bytes(act_slot.at[it, s], 7, act_send.at[it, s])
        wait_bytes(move_slot.at[it], 15, move_send.at[it])
        return carry

    lax.fori_loop(0, ITERS, drain, 0)


def place_outputs(first, rec, duals, weight, first_out, rec_out, dual_out, weight_out, sem):
    copies = [
        pltpu.make_async_copy(first, first_out, sem.at[0]),
        pltpu.make_async_copy(rec, rec_out, sem.at[1]),
        pltpu.make_async_copy(duals, dual_out, sem.at[2]),
        pltpu.make_async_copy(weight, weight_out, sem.at[3]),
    ]
    for copy in copies:
        copy.start()
    for copy in copies:
        copy.wait()


def local(
    tech_matrix,
    recourse_matrix,
    first_cost,
    recourse_cost,
    demand,
    first_upper,
    recourse_upper,
    first_start,
    recourse_start,
    dual_start,
):
    f32 = jnp.float32
    dma = pltpu.SemaphoreType.DMA
    first, rec, duals, weight = pl.pallas_call(
        kernel,
        out_shape=(
            jax.ShapeDtypeStruct((1, FIRST), f32),
            jax.ShapeDtypeStruct((SCEN, REC), f32),
            jax.ShapeDtypeStruct((SCEN, ROWS), f32),
            jax.ShapeDtypeStruct((1, 1), f32),
        ),
        in_specs=[pl.BlockSpec(memory_space=pltpu.HBM)] * 10,
        out_specs=[pl.BlockSpec(memory_space=pltpu.VMEM)] * 4,
        scratch_shapes=[
            pltpu.VMEM((SCEN, ROWS, COLS), jnp.bfloat16),
            pltpu.VMEM((SCEN, COLS, ROWS), jnp.bfloat16),
            pltpu.VMEM((1, FIRST), f32),
            pltpu.VMEM((SCEN, REC), f32),
            pltpu.VMEM((SCEN, ROWS), f32),
            pltpu.VMEM((1, FIRST), f32),
            pltpu.VMEM((SCEN, REC), f32),
            pltpu.VMEM((SCEN, 2 * SCEN, ROWS), f32),
            pltpu.VMEM((1, TRAIL), f32),
            pltpu.VMEM((SCEN, WIDE), f32),
            pltpu.VMEM((1, FIRST), f32),
            pltpu.VMEM((ITERS, 16, 1, FIRST), f32),
            pltpu.VMEM((ITERS, 3, 4, SCEN, WIDE), f32),
            pltpu.VMEM((ITERS, SCEN, 8, 1, ROWS + TRAIL), f32),
            pltpu.VMEM((ITERS, 16, 2, TRAIL), f32),
            dma((4, SCEN)),
            dma((8,)),
            dma((ITERS,)),
            dma((ITERS,)),
            dma((ITERS, 3)),
            dma((ITERS, 3)),
            dma((ITERS, SCEN)),
            dma((ITERS, SCEN)),
            dma((ITERS,)),
            dma((ITERS,)),
        ],
        compiler_params=pltpu.CompilerParams(
            collective_id=0, has_side_effects=True, vmem_limit_bytes=44 * 2**20
        ),
    )(
        *(
            pltpu.with_memory_space_constraint(array, pltpu.HBM)
            for array in (
                tech_matrix,
                recourse_matrix,
                first_cost.reshape(1, FIRST),
                recourse_cost,
                demand,
                first_upper.reshape(1, FIRST),
                recourse_upper,
                first_start.reshape(1, FIRST),
                recourse_start,
                dual_start,
            )
        )
    )
    outs = pl.pallas_call(
        place_outputs,
        out_shape=(
            jax.ShapeDtypeStruct((1, FIRST), f32),
            jax.ShapeDtypeStruct((SCEN, REC), f32),
            jax.ShapeDtypeStruct((SCEN, ROWS), f32),
            jax.ShapeDtypeStruct((1, 1), f32),
        ),
        in_specs=[pl.BlockSpec(memory_space=pl.ANY)] * 4,
        out_specs=[pl.BlockSpec(memory_space=pltpu.HBM)] * 4,
        scratch_shapes=[dma((4,))],
        compiler_params=pltpu.CompilerParams(vmem_limit_bytes=1 * 2**20),
    )(first, rec, duals, weight)
    return outs[0].reshape(FIRST), outs[1], outs[2], outs[3].reshape(())


def solution(mesh):
    in_specs = (
        P("scen", "row", "col"),
        P("scen", "row", "col"),
        P("col"),
        P("scen", "col"),
        P("scen", "row"),
        P("col"),
        P("scen", "col"),
        P("col"),
        P("scen", "col"),
        P("scen", "row"),
    )
    out_specs = (P("col"), P("scen", "col"), P("scen", "row"), P())
    return jax.shard_map(local, mesh=mesh, in_specs=in_specs, out_specs=out_specs, check_vma=False)
```

```python
import jax
import jax.numpy as jnp
from jax import lax
from jax.experimental import pallas as pl
from jax.experimental.pallas import tpu as pltpu
from jax.sharding import PartitionSpec as P

MESH = pl.DeviceIdType.MESH
ITERS = 4
STEP_SCALE = 0.8
EPSILON = 1e-06
SCEN, ROWS, FIRST, REC = 2, 2048, 512, 1536
COLS = FIRST + REC
WIDE = 512
PLACE = (2, 0, 1, 3)
TRAIL = 128
AHEAD = 3
EARLY = ((0, 0), (0, 1), (1, 0), (1, 1), (2, 0))


def split_rows(value):
    upper = value.astype(jnp.bfloat16).astype(jnp.float32)
    return jnp.concatenate([upper, value - upper], 0).astype(jnp.bfloat16)


def kernel(
    tech_hbm,
    rec_hbm,
    first_cost_hbm,
    rec_cost_hbm,
    demand_hbm,
    first_upper_hbm,
    rec_upper_hbm,
    first_start_hbm,
    rec_start_hbm,
    dual_start_hbm,
    first_now,
    rec_now,
    duals,
    weight_out,
    mat,
    mat_t,
    first_cost,
    rec_cost,
    demand,
    first_upper,
    rec_upper,
    sums,
    weight,
    tech_part,
    tech_slot,
    rec_slot,
    act_slot,
    move_slot,
    load_sem,
    small_sem,
    tech_send,
    tech_recv,
    rec_send,
    rec_recv,
    act_send,
    act_recv,
    move_send,
    move_recv,
):
    scen, row, col = lax.axis_index("scen"), lax.axis_index("row"), lax.axis_index("col")
    place = scen * 4 + row

    row_peers = [{"row": lax.rem(row + d, 4)} for d in (2, 1, 3)]
    col_peers = [{"col": lax.rem(col + d, 8)} for d in (4, 5, 3, 2, 6, 1, 7)]
    block_peers = [
        {"scen": lax.rem(scen + d, 4), "row": lax.rem(row + e, 4)}
        for d in (2, 1, 3, 0)
        for e in (2, 1, 3, 0)
        if d or e
    ]

    barrier = pltpu.get_barrier_semaphore()
    for peer in block_peers + col_peers:
        pl.semaphore_signal(barrier, inc=1, device_id=peer, device_id_type=MESH)

    pieces = []
    for part in range(4):
        for s in range(SCEN):
            if part == 0:
                source = tech_hbm.at[s]
            else:
                source = rec_hbm.at[s, :, pl.ds((part - 1) * WIDE, WIDE)]
            pieces.append(
                pltpu.make_async_copy(
                    source, mat.at[s, :, pl.ds(PLACE[part] * WIDE, WIDE)], load_sem.at[part, s]
                )
            )
    smalls = [
        pltpu.make_async_copy(dual_start_hbm, duals, small_sem.at[0]),
        pltpu.make_async_copy(demand_hbm, demand, small_sem.at[1]),
        pltpu.make_async_copy(rec_cost_hbm, rec_cost, small_sem.at[2]),
        pltpu.make_async_copy(rec_upper_hbm, rec_upper, small_sem.at[3]),
        pltpu.make_async_copy(rec_start_hbm, rec_now, small_sem.at[4]),
        pltpu.make_async_copy(first_cost_hbm, first_cost, small_sem.at[5]),
        pltpu.make_async_copy(first_upper_hbm, first_upper, small_sem.at[6]),
        pltpu.make_async_copy(first_start_hbm, first_now, small_sem.at[7]),
    ]
    for copy in smalls[:1] + pieces[:AHEAD] + smalls[1:]:
        copy.start()

    def send(slot, mine, peers, send_sem, recv_sem):
        for peer in peers:
            pltpu.make_async_remote_copy(
                src_ref=slot.at[mine],
                dst_ref=slot.at[mine],
                send_sem=send_sem,
                recv_sem=recv_sem,
                device_id=peer,
                device_id_type=MESH,
            ).start()

    def wait_bytes(slot, count, sem):
        view = slot.at[pl.ds(0, count)]
        pltpu.make_async_copy(view, view, sem).wait()

    def back(left, s, part):
        out = jnp.dot(
            left,
            mat[s, :, pl.ds(PLACE[part] * WIDE, WIDE)],
            preferred_element_type=jnp.float32,
        )
        return out[0:1] + out[1:2]

    def send_tech(it, total):
        tech_slot[it, pl.ds(place, 1)] = total.reshape(1, 1, WIDE)
        send(tech_slot.at[it], place, block_peers, tech_send.at[it], tech_recv.at[it])

    def send_rec(it, part):
        send(
            rec_slot.at[it, part - 1],
            row,
            row_peers,
            rec_send.at[it, part - 1],
            rec_recv.at[it, part - 1],
        )

    def turn(s, part):
        for k in range(2):
            cols = pl.ds(PLACE[part] * WIDE + k * 256, 256)
            mat_t[s, cols, :] = mat[s, :, cols].T

    smalls[0].wait()
    weight[...] = jnp.zeros_like(weight)
    left = [split_rows(duals[s : s + 1, :]) for s in range(SCEN)]
    total = None
    for part in range(4):
        for s in range(SCEN):
            pieces[part * 2 + s].wait()
            if part * 2 + s + AHEAD < len(pieces):
                pieces[part * 2 + s + AHEAD].start()
            out = back(left[s], s, part)
            if part == 0:
                total = out if s == 0 else total + out
            else:
                rec_slot[0, part - 1, row, pl.ds(s, 1)] = out
            if (part, s) in EARLY:
                turn(s, part)
        if part == 0:
            pl.semaphore_wait(barrier, 22)
            send_tech(0, total)
        else:
            send_rec(0, part)
    for part in (1, 2, 0, 3):
        for s in range(SCEN):
            if (part, s) not in EARLY:
                turn(s, part)
    for copy in smalls[1:]:
        copy.wait()

    def forward(bar, s, first, count):
        return jnp.dot(
            split_rows(bar),
            mat_t[s, pl.ds(first * WIDE, count * WIDE), :],
            preferred_element_type=jnp.float32,
        )

    def wide(value, count):
        return jnp.concatenate([value] * (count // TRAIL), 1)

    def iterate(it, carry):
        log_weight = weight[...]
        step_primal = wide(STEP_SCALE * jnp.exp(-log_weight), WIDE)
        step_dual = wide(STEP_SCALE * jnp.exp(log_weight), ROWS)

        def rec_step(part):
            wait_bytes(rec_slot.at[it, part - 1], 3, rec_recv.at[it, part - 1])
            grad = rec_slot[it, part - 1, 0]
            for p in range(1, 4):
                grad = grad + rec_slot[it, part - 1, p]
            cols = pl.ds((part - 1) * WIDE, WIDE)
            old = rec_now[:, cols]
            new = jnp.clip(
                old - step_primal * (rec_cost[:, cols] - grad), 0.0, rec_upper[:, cols]
            )
            rec_now[:, cols] = new
            square = 0.25 * (new - old) ** 2
            return 2.0 * new - old, square[0:1] + square[1:2]

        def first_step():
            wait_bytes(tech_slot.at[it], 15, tech_recv.at[it])
            grad = tech_slot[it, 0]
            for p in range(1, 16):
                grad = grad + tech_slot[it, p]
            old = first_now[...]
            new = jnp.clip(old - step_primal * (first_cost[...] - grad), 0.0, first_upper[...])
            first_now[...] = new
            return jnp.broadcast_to(2.0 * new - old, (SCEN, FIRST)), 0.0625 * (new - old) ** 2

        bar, move = rec_step(1)
        for s in range(SCEN):
            sums[s] = forward(bar, s, 0, 1)
        bar_2, move_2 = rec_step(2)
        bar_0, move_0 = first_step()
        bar = jnp.concatenate([bar_2, bar_0], 1)
        move = move + move_2 + move_0
        for s in range(SCEN):
            sums[s] = sums[s] + forward(bar, s, 1, 2)
        bar, move_3 = rec_step(3)
        move = move + move_3
        spread = move[:, 0:TRAIL]
        for k in range(1, WIDE // TRAIL):
            spread = spread + move[:, k * TRAIL : (k + 1) * TRAIL]
        for s in range(SCEN):
            act_slot[it, s, col, :, pl.ds(ROWS, TRAIL)] = spread
            out = sums[s] + forward(bar, s, 3, 1)
            act_slot[it, s, col, :, pl.ds(0, ROWS)] = out[s : s + 1] + out[2 + s : 3 + s]
            send(act_slot.at[it, s], col, col_peers, act_send.at[it, s], act_recv.at[it, s])

        def dual_step(s):
            wait_bytes(act_slot.at[it, s], 7, act_recv.at[it, s])
            activity = act_slot[it, s, 0]
            for p in range(1, 8):
                activity = activity + act_slot[it, s, p]
            old = duals[s : s + 1, :]
            new = jnp.maximum(
                0.0, old + step_dual * (demand[s : s + 1, :] - activity[:, :ROWS])
            )
            duals[s : s + 1, :] = new
            square = (new - old) ** 2
            spread = square[:, 0:TRAIL]
            for k in range(1, ROWS // TRAIL):
                spread = spread + square[:, k * TRAIL : (k + 1) * TRAIL]
            return new, spread, activity[:, ROWS:]

        new_0, spread_0, _ = dual_step(0)
        left_0 = split_rows(new_0)
        tech_part[...] = back(left_0, 0, 0)
        new_1, spread_1, primal = dual_step(1)
        move_slot[it, pl.ds(place, 1)] = jnp.concatenate([spread_0 + spread_1, primal], 0).reshape(
            1, 2, TRAIL
        )
        send(move_slot.at[it], place, block_peers, move_send.at[it], move_recv.at[it])

        @pl.when(it < ITERS - 1)
        def _():
            left = [split_rows(duals[s : s + 1, :]) for s in range(SCEN)]
            send_tech(it + 1, tech_part[...] + back(left[1], 1, 0))
            for part in (1, 2, 3):
                for s in range(SCEN):
                    rec_slot[it + 1, part - 1, row, pl.ds(s, 1)] = back(left[s], s, part)
                send_rec(it + 1, part)

        wait_bytes(move_slot.at[it], 15, move_recv.at[it])
        moves = move_slot[it, 0]
        for p in range(1, 16):
            moves = moves + move_slot[it, p]
        logs = jnp.log(jnp.broadcast_to(jnp.sum(moves, 1, keepdims=True), (2, TRAIL)) + EPSILON)
        weight[...] = 0.25 * (logs[0:1] - logs[1:2]) + 0.5 * log_weight
        return carry

    lax.fori_loop(0, ITERS, iterate, 0)

    weight_out[...] = jnp.exp(weight[:, 0:1])

    def drain(it, carry):
        wait_bytes(tech_slot.at[it], 15, tech_send.at[it])
        for part in range(3):
            wait_bytes(rec_slot.at[it, part], 3, rec_send.at[it, part])
        for s in range(SCEN):
            wait_bytes(act_slot.at[it, s], 7, act_send.at[it, s])
        wait_bytes(move_slot.at[it], 15, move_send.at[it])
        return carry

    lax.fori_loop(0, ITERS, drain, 0)


def place_outputs(first, rec, duals, weight, first_out, rec_out, dual_out, weight_out, sem):
    copies = [
        pltpu.make_async_copy(first, first_out, sem.at[0]),
        pltpu.make_async_copy(rec, rec_out, sem.at[1]),
        pltpu.make_async_copy(duals, dual_out, sem.at[2]),
        pltpu.make_async_copy(weight, weight_out, sem.at[3]),
    ]
    for copy in copies:
        copy.start()
    for copy in copies:
        copy.wait()


def local(
    tech_matrix,
    recourse_matrix,
    first_cost,
    recourse_cost,
    demand,
    first_upper,
    recourse_upper,
    first_start,
    recourse_start,
    dual_start,
):
    f32 = jnp.float32
    dma = pltpu.SemaphoreType.DMA
    first, rec, duals, weight = pl.pallas_call(
        kernel,
        out_shape=(
            jax.ShapeDtypeStruct((1, FIRST), f32),
            jax.ShapeDtypeStruct((SCEN, REC), f32),
            jax.ShapeDtypeStruct((SCEN, ROWS), f32),
            jax.ShapeDtypeStruct((1, 1), f32),
        ),
        in_specs=[pl.BlockSpec(memory_space=pltpu.HBM)] * 10,
        out_specs=[pl.BlockSpec(memory_space=pltpu.VMEM)] * 4,
        scratch_shapes=[
            pltpu.VMEM((SCEN, ROWS, COLS), jnp.bfloat16),
            pltpu.VMEM((SCEN, COLS, ROWS), jnp.bfloat16),
            pltpu.VMEM((1, FIRST), f32),
            pltpu.VMEM((SCEN, REC), f32),
            pltpu.VMEM((SCEN, ROWS), f32),
            pltpu.VMEM((1, FIRST), f32),
            pltpu.VMEM((SCEN, REC), f32),
            pltpu.VMEM((SCEN, 2 * SCEN, ROWS), f32),
            pltpu.VMEM((1, TRAIL), f32),
            pltpu.VMEM((1, FIRST), f32),
            pltpu.VMEM((ITERS, 16, 1, FIRST), f32),
            pltpu.VMEM((ITERS, 3, 4, SCEN, WIDE), f32),
            pltpu.VMEM((ITERS, SCEN, 8, 1, ROWS + TRAIL), f32),
            pltpu.VMEM((ITERS, 16, 2, TRAIL), f32),
            dma((4, SCEN)),
            dma((8,)),
            dma((ITERS,)),
            dma((ITERS,)),
            dma((ITERS, 3)),
            dma((ITERS, 3)),
            dma((ITERS, SCEN)),
            dma((ITERS, SCEN)),
            dma((ITERS,)),
            dma((ITERS,)),
        ],
        compiler_params=pltpu.CompilerParams(
            collective_id=0, has_side_effects=True, vmem_limit_bytes=44 * 2**20
        ),
    )(
        *(
            pltpu.with_memory_space_constraint(array, pltpu.HBM)
            for array in (
                tech_matrix,
                recourse_matrix,
                first_cost.reshape(1, FIRST),
                recourse_cost,
                demand,
                first_upper.reshape(1, FIRST),
                recourse_upper,
                first_start.reshape(1, FIRST),
                recourse_start,
                dual_start,
            )
        )
    )
    outs = pl.pallas_call(
        place_outputs,
        out_shape=(
            jax.ShapeDtypeStruct((1, FIRST), f32),
            jax.ShapeDtypeStruct((SCEN, REC), f32),
            jax.ShapeDtypeStruct((SCEN, ROWS), f32),
            jax.ShapeDtypeStruct((1, 1), f32),
        ),
        in_specs=[pl.BlockSpec(memory_space=pl.ANY)] * 4,
        out_specs=[pl.BlockSpec(memory_space=pltpu.HBM)] * 4,
        scratch_shapes=[dma((4,))],
        compiler_params=pltpu.CompilerParams(vmem_limit_bytes=1 * 2**20),
    )(first, rec, duals, weight)
    return outs[0].reshape(FIRST), outs[1], outs[2], outs[3].reshape(())


def solution(mesh):
    in_specs = (
        P("scen", "row", "col"),
        P("scen", "row", "col"),
        P("col"),
        P("scen", "col"),
        P("scen", "row"),
        P("col"),
        P("scen", "col"),
        P("col"),
        P("scen", "col"),
        P("scen", "row"),
    )
    out_specs = (P("col"), P("scen", "col"), P("scen", "row"), P())
    return jax.shard_map(local, mesh=mesh, in_specs=in_specs, out_specs=out_specs, check_vma=False)
```
